512 devices in a mesh: row: 8 (over y, z_hi), col: 8 (over x, core), depth: 8 (over z_lo).
Axes of the slice: x: 4, y: 4, z: 16 (z_hi: 2, z_lo: 8; z = z_hi * 8 + z_lo), core: 2. Of those that a mesh axis runs over, the one named last changes fastest.
Arguments:
- tokens: bfloat16 [512, 12288], P('col', 'row'), may hold values from -6 to 6
- weight_in: bfloat16 [12288, 49152], P('row', ('col', 'depth')), may hold values from -0.0546875 to 0.0546875
- bias_in: float32 [49152], P(('col', 'depth')), may hold values from -3 to 3
- weight_out: bfloat16 [49152, 12288], P(('col', 'depth'), 'row'), may hold values from -0.02734375 to 0.02734375
- bias_out: float32 [12288], P('row'), may hold values from -3 to 3
Outputs:
- layer_out: bfloat16 [512, 12288], P(('col', 'depth'), 'row')
The draws below stay inside these ranges and needn't reach their ends.
All inputs are finite; a program needn't handle non-finite values.
Results may differ from the reference program's by a relative error of at most 0.0045.
Values may be sent and summed in bfloat16 or wider, within the bound.
A program may use at most 64 MiB of HBM per device.

```python
import jax
import jax.numpy as jnp

D = 12288
FF = 49152
TOKENS = 512


def steps_of(own_key, dims, cuts, least, high):
    def one(position, blocks):
        draws = jax.random.uniform(jax.random.fold_in(jax.random.fold_in(own_key, 6), position), (blocks,), jnp.float32, least / len(cuts), high / len(cuts))
        return jnp.repeat(jnp.exp(draws), dims[position] // blocks).reshape((-1,) + (1,) * (len(dims) - position - 1))

    gain = one(*cuts[0])
    for cut in cuts[1:]:
        gain = gain * one(*cut)
    return gain


def noise(stream_key, dims, width, most, pieces=(), dtype=jnp.bfloat16):
    loudness = steps_of(stream_key, dims, pieces, -0.22, 0.18) if pieces else 1.0
    array = jax.random.normal(stream_key, dims, jnp.float32) * width * loudness
    return jnp.minimum(jnp.maximum(array, -most), most).astype(dtype)


def setup_inputs(seed: int = 0) -> dict:
    seeds = jax.random.split(jax.random.key(seed), 6)
    tokens = noise(seeds[0], (TOKENS, D), 1.0, 6.0, ((0, 8), (1, 8)))
    weight_in = noise(seeds[1], (D, FF), D ** -0.5, 0.0546875, ((0, 8), (1, 64)))
    bias_in = noise(seeds[2], (FF,), 0.5, 3.0, ((0, 64),), jnp.float32)
    weight_out = noise(seeds[3], (FF, D), FF ** -0.5, 0.02734375, ((0, 64), (1, 8)))
    bias_out = noise(seeds[4], (D,), 0.5, 3.0, ((0, 8),), jnp.float32)
    return {"tokens": tokens, "weight_in": weight_in, "bias_in": bias_in, "weight_out": weight_out, "bias_out": bias_out}


def reference(tokens, weight_in, bias_in, weight_out, bias_out):
    pre_act = jnp.dot(tokens, weight_in, preferred_element_type=jnp.float32) + bias_in
    hidden = jax.nn.gelu(pre_act, approximate=True).astype(jnp.bfloat16)
    summed = jnp.dot(hidden, weight_out, preferred_element_type=jnp.float32)
    return (summed + bias_out).astype(jnp.bfloat16)
```

```python
import jax
import jax.numpy as jnp
from jax import lax
from jax.experimental import pallas as pl
from jax.experimental.pallas import tpu as pltpu
from jax.sharding import PartitionSpec as P

CHUNKS = 4
TOKENS, WIDTH, UNITS = 512, 1536, 768
CHUNK = TOKENS // CHUNKS
MINE = CHUNK // 8
PIECE = CHUNK // 4
DEPTHS = MINE // 8
TILE = 256
HALF = WIDTH // 2


def remote(src, dst, send, recv, device):
    return pltpu.make_async_remote_copy(
        src_ref=src,
        dst_ref=dst,
        send_sem=send,
        recv_sem=recv,
        device_id=device,
        device_id_type=pl.DeviceIdType.MESH,
    )


def kernel(
    tokens, weight_in, bias_in, weight_out, bias_out, out,
    w_in, w_out, gathered, pre_send, pre_recv, pre_sum, pre_out, pre_other, hidden,
    total, total_other, x_send, x_recv, x_sum, z_send, z_recv,
    local_sem, tok_ss, tok_rs, sib_ss, sib_rs, pre_ss, pre_rs, half_ss, half_rs,
    hid_ss, hid_rs, core_ss, core_rs, x_ss, x_rs, z_ss, z_rs,
):
    row, col, depth = lax.axis_index("row"), lax.axis_index("col"), lax.axis_index("depth")
    y, z_hi, x, core = row // 2, row % 2, col // 2, col % 2

    def at_x(step):
        return {"col": ((x + step) % 4) * 2 + core}

    def at_y(step):
        return {"row": ((y + step) % 4) * 2 + z_hi}

    sibling = {"col": x * 2 + 1 - core}
    other_half = {"row": y * 2 + 1 - z_hi}

    def at_depth(d):
        return {"depth": d}

    own = pl.ds(pl.multiple_of(col * MINE, MINE), MINE)
    get_w_in = pltpu.make_async_copy(weight_in, w_in, local_sem.at[CHUNKS])
    get_w_out = pltpu.make_async_copy(weight_out, w_out, local_sem.at[CHUNKS + 1])
    get_own = [
        pltpu.make_async_copy(
            tokens.at[pl.ds(k * MINE, MINE)], gathered.at[k, own], local_sem.at[k]
        )
        for k in range(CHUNKS)
    ]
    for copy in get_own:
        copy.start()
    get_w_in.start()
    get_w_out.start()

    barrier = pltpu.get_barrier_semaphore()
    partners = [at_x(1), at_x(2), at_x(3), at_y(1), at_y(2), at_y(3), sibling, other_half]
    partners += [at_depth((depth + s) % 8) for s in range(1, 8)]
    for device in partners:
        pl.semaphore_signal(barrier, inc=1, device_id=device, device_id_type=pl.DeviceIdType.MESH)
    pl.semaphore_wait(barrier, len(partners))

    def tok_copy(k, s):
        return remote(
            tokens.at[pl.ds(k * MINE, MINE)], gathered.at[k, own],
            tok_ss.at[k, s - 1], tok_rs.at[k, s - 1], at_x(s),
        )

    def tok_place(step, which):
        c = ((x + 4 - step) % 4) * 2 + which
        return pl.ds(pl.multiple_of(c * MINE, MINE), MINE)

    def sib_copy(k, s, which):
        place = tok_place(s, which)
        src = tokens.at[pl.ds(k * MINE, MINE)] if s == 0 else gathered.at[k, place]
        return remote(src, gathered.at[k, place], sib_ss.at[k, s], sib_rs.at[k, s], sibling)

    def pre_copy(k, s):
        piece = pl.ds(pl.multiple_of(((y + s) % 4) * PIECE, PIECE), PIECE)
        return remote(
            pre_send.at[k, piece], pre_recv.at[k, s - 1],
            pre_ss.at[k, s - 1], pre_rs.at[k, s - 1], at_y(s),
        )

    def half_copy(k):
        return remote(pre_out.at[k], pre_other.at[k], half_ss.at[k], half_rs.at[k], other_half)

    my_piece = pl.ds(pl.multiple_of(y * PIECE, PIECE), PIECE)

    def hid_copy(k, s):
        return remote(
            hidden.at[k, my_piece], hidden.at[k, my_piece],
            hid_ss.at[k, s - 1], hid_rs.at[k, s - 1], at_y(s),
        )

    def core_copy(k, i):
        rows = pl.ds(pl.multiple_of((2 * i + 1 - core) * MINE, MINE), MINE)
        return remote(
            total.at[k, rows], total_other.at[k, i], core_ss.at[k, i], core_rs.at[k, i], sibling
        )

    def x_copy(k, s):
        return remote(
            x_send.at[k, s - 1], x_recv.at[k, s - 1], x_ss.at[k, s - 1], x_rs.at[k, s - 1], at_x(s)
        )

    def z_copy(d, to):
        return remote(z_send.at[d], z_recv.at[depth], z_ss.at[d], z_rs.at[depth], at_depth(to))

    def forward(k):
        for s in range(1, 4):
            tok_copy(k, s).wait_recv()
            sib_copy(k, s, core).start()

    def first_product(k):
        get_own[k].wait()
        for s in range(4):
            sib_copy(k, s, 1 - core).wait_recv()
        if k == 0:
            get_w_in.wait()

        def tile(i, _):
            units = pl.ds(pl.multiple_of(i * TILE, TILE), TILE)
            part = jnp.dot(gathered[k], w_in[:, units], preferred_element_type=jnp.float32)
            pre_send[k, :, units] = part.astype(jnp.bfloat16)
            pre_sum[:, units] = part
            return 0

        lax.fori_loop(0, UNITS // TILE, tile, 0)
        for s in range(1, 4):
            pre_copy(k, s).start()
        keep[k] = pre_sum[my_piece, :]

    keep = {}

    def sum_pieces(k):
        acc = keep.pop(k)
        for s in range(1, 4):
            pre_copy(k, s).wait_recv()
            acc = acc + pre_recv[k, s - 1].astype(jnp.float32)
        pre_out[k] = acc.astype(jnp.bfloat16)
        half_copy(k).start()
        keep[k] = acc

    def activate(k):
        half_copy(k).wait_recv()
        v = keep.pop(k) + pre_other[k].astype(jnp.float32) + bias_in[...]
        hidden[k, my_piece, :] = jax.nn.gelu(v, approximate=True).astype(jnp.bfloat16)
        for s in range(1, 4):
            hid_copy(k, s).start()

    def second_product(k):
        for s in range(1, 4):
            hid_copy(k, s).wait_recv()
        if k == 0:
            get_w_out.wait()

        def tile(i, _):
            cols = pl.ds(pl.multiple_of(i * TILE, TILE), TILE)
            total[k, :, cols] = jnp.dot(
                hidden[k], w_out[:, cols], preferred_element_type=jnp.float32
            )
            return 0

        lax.fori_loop(0, WIDTH // TILE, tile, 0)
        for i in range(4):
            core_copy(k, i).start()

    def sum_cores(k):
        for i in range(4):
            core_copy(k, i).wait_recv()
        for s in (1, 2, 3, 0):
            i = (x + s) % 4
            rows = pl.ds(pl.multiple_of((2 * i + core) * MINE, MINE), MINE)
            part = total[k, rows, :] + total_other[k, i]
            if s:
                x_send[k, s - 1] = part.astype(jnp.bfloat16)
                x_copy(k, s).start()
            else:
                x_sum[k] = part

    def sum_x(k):
        acc = x_sum[k]
        for s in range(1, 4):
            x_copy(k, s).wait_recv()
            acc = acc + x_recv[k, s - 1].astype(jnp.float32)
        for n in range(DEPTHS):
            d = k * DEPTHS + n
            part = acc[n * 8:(n + 1) * 8]
            folded = jnp.concatenate([part[:, :HALF], part[:, HALF:]], axis=0)

            @pl.when(depth == d)
            def _():
                out[...] = part

            @pl.when(depth != d)
            def _():
                z_send[d] = folded.astype(jnp.bfloat16)
                z_copy(d, d).start()

    for k in range(CHUNKS):
        for s in (2, 1, 3):
            tok_copy(k, s).start()
        sib_copy(k, 0, core).start()

    stages = (
        (forward, 0.0, 2.0), (first_product, 1.0, 2.0), (sum_pieces, 5.0, 2.0), (activate, 10.0, 4.5),
        (second_product, 13.0, 4.5), (sum_cores, 14.5, 4.5), (sum_x, 17.5, 4.5),
    )
    order = sorted(
        (start + k * gap, n, k) for n, (_, start, gap) in enumerate(stages) for k in range(CHUNKS)
    )
    for _, n, k in order:
        stages[n][0](k)

    acc = out[...] + bias_out[...]
    for s in range(1, 8):
        d = (depth + s) % 8
        remote(z_send.at[d], z_recv.at[d], z_ss.at[d], z_rs.at[d], at_depth(d)).wait_recv()
        part = z_recv[d].astype(jnp.float32)
        acc = acc + jnp.concatenate([part[:8], part[8:]], axis=1)
    out[...] = acc

    for k in range(CHUNKS):
        for s in range(1, 4):
            tok_copy(k, s).wait_send()
            pre_copy(k, s).wait_send()
            hid_copy(k, s).wait_send()
            x_copy(k, s).wait_send()
        for s in range(4):
            sib_copy(k, s, core).wait_send()
            core_copy(k, s).wait_send()
        half_copy(k).wait_send()
    for d in range(8):
        @pl.when(depth != d)
        def _():
            z_copy(d, d).wait_send()


def on_device(tokens, weight_in, bias_in, weight_out, bias_out):
    bf16, f32 = jnp.bfloat16, jnp.float32
    dma = pltpu.SemaphoreType.DMA
    vmem = pltpu.VMEM
    summed = pl.pallas_call(
        kernel,
        out_shape=jax.ShapeDtypeStruct((8, WIDTH), f32),
        in_specs=[
            pl.BlockSpec(memory_space=pl.ANY),
            pl.BlockSpec(memory_space=pl.ANY),
            pl.BlockSpec(memory_space=pltpu.VMEM),
            pl.BlockSpec(memory_space=pl.ANY),
            pl.BlockSpec(memory_space=pltpu.VMEM),
        ],
        out_specs=pl.BlockSpec(memory_space=pltpu.VMEM),
        scratch_shapes=[
            vmem((WIDTH, UNITS), bf16),
            vmem((UNITS, WIDTH), bf16),
            vmem((CHUNKS, CHUNK, WIDTH), bf16),
            vmem((CHUNKS, CHUNK, UNITS), bf16),
            vmem((CHUNKS, 3, PIECE, UNITS), bf16),
            vmem((CHUNK, UNITS), f32),
            vmem((CHUNKS, PIECE, UNITS), bf16),
            vmem((CHUNKS, PIECE, UNITS), bf16),
            vmem((CHUNKS, CHUNK, UNITS), bf16),
            vmem((CHUNKS, CHUNK, WIDTH), f32),
            vmem((CHUNKS, 4, MINE, WIDTH), f32),
            vmem((CHUNKS, 3, MINE, WIDTH), bf16),
            vmem((CHUNKS, 3, MINE, WIDTH), bf16),
            vmem((CHUNKS, MINE, WIDTH), f32),
            vmem((8, 16, HALF), bf16),
            vmem((8, 16, HALF), bf16),
            dma((CHUNKS + 2,)),
            dma((CHUNKS, 3)), dma((CHUNKS, 3)),
            dma((CHUNKS, 4)), dma((CHUNKS, 4)),
            dma((CHUNKS, 3)), dma((CHUNKS, 3)),
            dma((CHUNKS,)), dma((CHUNKS,)),
            dma((CHUNKS, 3)), dma((CHUNKS, 3)),
            dma((CHUNKS, 4)), dma((CHUNKS, 4)),
            dma((CHUNKS, 3)), dma((CHUNKS, 3)),
            dma((8,)), dma((8,)),
        ],
        compiler_params=pltpu.CompilerParams(
            collective_id=0, has_side_effects=True, vmem_limit_bytes=40 * 2**20
        ),
        cost_estimate=pl.CostEstimate(
            flops=4 * TOKENS * WIDTH * UNITS, bytes_accessed=4 * WIDTH * UNITS, transcendentals=0
        ),
        name="feed_forward",
    )(tokens, weight_in, bias_in.reshape(1, UNITS), weight_out, bias_out.reshape(1, WIDTH))
    return summed.astype(jnp.bfloat16)


def solution(mesh):
    placed = (
        P("col", "row"),
        P("row", ("col", "depth")),
        P(("col", "depth")),
        P(("col", "depth"), "row"),
        P("row"),
    )
    return jax.shard_map(
        on_device, mesh=mesh, in_specs=placed, out_specs=P(("col", "depth"), "row"), check_vma=False
    )
```

```python
import jax
import jax.numpy as jnp
from jax import lax
from jax.experimental import pallas as pl
from jax.experimental.pallas import tpu as pltpu
from jax.sharding import PartitionSpec as P

PARTS = ((0, None), (1, None), (2, None), (3, None))
N = len(PARTS)
TOKENS, WIDTH, UNITS = 512, 1536, 768
MINE = 16
SIDE = 4 * MINE
SIZES = [SIDE if e is not None else 2 * SIDE for _, e in PARTS]
BASES = [sum(SIZES[:k]) for k in range(N)]
PIECES = [size // 4 for size in SIZES]
TILE = 256
PACE = 1
HALF = WIDTH // 2


def schedule():
    order = []
    for t in range(N + 1):
        if t < N:
            order += [("gather", t), ("first_product", t)]
        if t >= 1:
            order += [("sum_pieces", t - 1)]
    for t in range(N + 3):
        for lag, stage in enumerate(("activate", "second_product", "sum_cores", "sum_x")):
            if 0 <= t - lag < N:
                order += [(stage, t - lag)]
    return order


def remote(src, dst, send, recv, device):
    return pltpu.make_async_remote_copy(
        src_ref=src,
        dst_ref=dst,
        send_sem=send,
        recv_sem=recv,
        device_id=device,
        device_id_type=pl.DeviceIdType.MESH,
    )


def kernel(
    tokens, weight_in, bias_in, weight_out, bias_out, out,
    w_in, w_out, b_in, b_out, gathered, pre_send, pre_recv, pre_sum, pre_out, pre_other, hidden,
    total, total_other, x_send, x_recv, x_sum, z_send, z_recv,
    local_sem, tok_ss, tok_rs, sib_ss, sib_rs, pre_ss, pre_rs, half_ss, half_rs,
    hid_ss, hid_rs, core_ss, core_rs, x_ss, x_rs, z_ss, z_rs, half_ready, depth_ready,
):
    row, col, depth = lax.axis_index("row"), lax.axis_index("col"), lax.axis_index("depth")
    y, z_hi, x, core = row // 2, row % 2, col // 2, col % 2

    def at_x(step):
        return {"col": ((x + step) % 4) * 2 + core}

    def at_y(step):
        return {"row": ((y + step) % 4) * 2 + z_hi}

    sibling = {"col": x * 2 + 1 - core}
    other_half = {"row": y * 2 + 1 - z_hi}

    def at_depth(d):
        return {"depth": d}

    def on_core(e, body):
        if e is None:
            body()
        else:
            pl.when(core == e)(body)

    def rows(start, size):
        return pl.ds(pl.multiple_of(start, 16), size)

    def core_rows(k, which):
        return rows(BASES[k] + (which * SIDE if PARTS[k][1] is None else 0), SIDE)

    def own_rows(k):
        return rows(BASES[k] + (core * SIDE if PARTS[k][1] is None else 0) + x * MINE, MINE)

    get_w_in = pltpu.make_async_copy(weight_in, w_in, local_sem.at[N])
    get_w_out = pltpu.make_async_copy(weight_out, w_out, local_sem.at[N + 1])
    get_b_in = pltpu.make_async_copy(bias_in, b_in.at[0], local_sem.at[N + 2])
    get_b_out = pltpu.make_async_copy(bias_out, b_out.at[0], local_sem.at[N + 3])
    get_own = [
        pltpu.make_async_copy(
            tokens.at[pl.ds(q * MINE, MINE)], gathered.at[own_rows(k)], local_sem.at[k]
        )
        for k, (q, _) in enumerate(PARTS)
    ]
    for k, (_, e) in enumerate(PARTS):
        on_core(e, get_own[k].start)
    get_w_in.start()
    get_b_in.start()

    def signal(semaphore, device):
        pl.semaphore_signal(
            semaphore, inc=1, device_id=device, device_id_type=pl.DeviceIdType.MESH
        )

    barrier = pltpu.get_barrier_semaphore()
    near = [at_x(1), at_x(2), at_x(3), at_y(1), at_y(2), at_y(3), sibling]
    for device in near:
        signal(barrier, device)

    @pl.when(z_hi == 0)
    def _():
        signal(barrier, other_half)

    for d in range(1, 8):
        @pl.when(depth < d)
        def _():
            signal(barrier, at_depth(d))

    pl.semaphore_wait(barrier, len(near) + z_hi + depth)

    def tok_copy(k, s):
        src = tokens.at[pl.ds(PARTS[k][0] * MINE, MINE)]
        return remote(src, gathered.at[own_rows(k)], tok_ss.at[k], tok_rs.at[k], at_x(s))

    def tok_all(k):
        place = gathered.at[pl.ds(BASES[k], 3 * MINE)]
        return remote(place, place, tok_ss.at[k], tok_rs.at[k], at_x(1))

    def sib_copy(k, which):
        place = gathered.at[core_rows(k, which)]
        return remote(place, place, sib_ss.at[k], sib_rs.at[k], sibling)

    def pre_slot(k, s):
        return pre_recv.at[pl.ds(BASES[k] // 4 * 3 + (s - 1) * PIECES[k], PIECES[k])]

    def pre_copy(k, s):
        piece = rows(BASES[k] + ((y + s) % 4) * PIECES[k], PIECES[k])
        return remote(pre_send.at[piece], pre_slot(k, s), pre_ss.at[k], pre_rs.at[k], at_y(s))

    def pre_all(k):
        place = pre_recv.at[pl.ds(BASES[k] // 4 * 3, 3 * PIECES[k])]
        return remote(place, place, pre_ss.at[k], pre_rs.at[k], at_y(1))

    def half_copy(k):
        piece = pl.ds(BASES[k] // 4, PIECES[k])
        return remote(
            pre_out.at[piece], pre_other.at[piece], half_ss.at[k], half_rs.at[k], other_half
        )

    def my_piece(k):
        return rows(BASES[k] + y * PIECES[k], PIECES[k])

    def hid_copy(k, s):
        place = hidden.at[my_piece(k)]
        return remote(place, place, hid_ss.at[k], hid_rs.at[k], at_y(s))

    def hid_all(k):
        place = hidden.at[pl.ds(BASES[k], 3 * PIECES[k])]
        return remote(place, place, hid_ss.at[k], hid_rs.at[k], at_y(1))

    def core_copy(k):
        return remote(
            total.at[core_rows(k, 1 - core)], total_other.at[k], core_ss.at[k], core_rs.at[k], sibling
        )

    def x_copy(k, s):
        return remote(x_send.at[k, s - 1], x_recv.at[k, s - 1], x_ss.at[k], x_rs.at[k], at_x(s))

    def x_all(k):
        return remote(x_send.at[k], x_recv.at[k], x_ss.at[k], x_rs.at[k], at_x(1))

    def z_copy(d, to):
        return remote(z_send.at[d], z_recv.at[depth], z_ss.at[d], z_rs, at_depth(to))

    def gather(k):
        e = PARTS[k][1]

        def body():
            get_own[k].wait()
            tok_all(k).wait_recv()
            sib_copy(k, core).start()

        on_core(e, body)

    def first_product(k):
        e = PARTS[k][1]
        on_core(None if e is None else 1 - e, lambda: sib_copy(k, 1 - core).wait_recv())
        if k == 0:
            get_w_in.wait()
            get_b_in.wait()
        part_rows = pl.ds(BASES[k], SIZES[k])

        def tile(i, _):
            units = pl.ds(pl.multiple_of(i * TILE, TILE), TILE)
            part = jnp.dot(
                gathered[part_rows, :], w_in[:, units], preferred_element_type=jnp.float32
            )
            pre_send[part_rows, units] = part.astype(jnp.bfloat16)
            pre_sum[part_rows, units] = part
            return 0

        lax.fori_loop(0, UNITS // TILE, tile, 0)
        for s in range(1, 4):
            pre_copy(k, s).start()

    def sum_pieces(k):
        acc = pre_sum[my_piece(k), :]
        pre_all(k).wait_recv()
        for s in range(1, 4):
            acc = acc + pre_slot(k, s)[...].astype(jnp.float32)
        pre_out[pl.ds(BASES[k] // 4, PIECES[k]), :] = acc.astype(jnp.bfloat16)
        if k == 0:
            @pl.when(z_hi == 0)
            def _():
                pl.semaphore_wait(half_ready, 1)

        if PACE and k >= PACE:
            half_copy(k - PACE).wait_send()
        half_copy(k).start()
        pre_sum[my_piece(k), :] = acc

    def activate(k):
        acc = pre_sum[my_piece(k), :] + b_in[...]
        half_copy(k).wait_recv()
        v = acc + pre_other[pl.ds(BASES[k] // 4, PIECES[k]), :].astype(jnp.float32)
        hidden[my_piece(k), :] = jax.nn.gelu(v, approximate=True).astype(jnp.bfloat16)
        for s in range(1, 4):
            hid_copy(k, s).start()

    def second_product(k):
        hid_all(k).wait_recv()
        if k == 0:
            get_w_out.wait()
            get_b_out.wait()
        part_rows = pl.ds(BASES[k], SIZES[k])

        def tile(i, _):
            cols = pl.ds(pl.multiple_of(i * TILE, TILE), TILE)
            total[part_rows, cols] = jnp.dot(
                hidden[part_rows, :], w_out[:, cols], preferred_element_type=jnp.float32
            )
            return 0

        lax.fori_loop(0, WIDTH // TILE, tile, 0)
        e = PARTS[k][1]
        on_core(None if e is None else 1 - e, lambda: core_copy(k).start())

    def sum_cores(k):
        e = PARTS[k][1]
        first = BASES[k] + (core * SIDE if e is None else 0)

        def body():
            core_copy(k).wait_recv()
            for s in (2, 1, 3, 0):
                i = (x + s) % 4
                part = total[rows(first + i * MINE, MINE), :] + total_other[k, rows(i * MINE, MINE), :]
                if s:
                    x_send[k, s - 1] = part.astype(jnp.bfloat16)
                    x_copy(k, s).start()
                else:
                    x_sum[k] = part

        on_core(e, body)

    def sum_x(k):
        q, e = PARTS[k]
        if k == 0:
            @pl.when(depth < 7)
            def _():
                pl.semaphore_wait(depth_ready, 7 - depth)

        def body():
            acc = x_sum[k]
            x_all(k).wait_recv()
            for s in range(1, 4):
                acc = acc + x_recv[k, s - 1].astype(jnp.float32)
            for n in range(2):
                d = 2 * q + n
                part = acc[n * 8:(n + 1) * 8]
                folded = jnp.concatenate([part[:, :HALF], part[:, HALF:]], axis=0)

                @pl.when(depth == d)
                def _():
                    out[...] = part

                @pl.when(depth != d)
                def _():
                    z_send[d] = folded.astype(jnp.bfloat16)
                    z_copy(d, d).start()

        on_core(e, body)

    def send_tokens(k):
        for s in (2, 1, 3):
            tok_copy(k, s).start()

    for k, (_, e) in enumerate(PARTS):
        on_core(e, lambda: send_tokens(k))

    @pl.when(z_hi == 1)
    def _():
        signal(half_ready, other_half)

    for d in range(7):
        @pl.when(depth > d)
        def _():
            signal(depth_ready, at_depth(d))

    get_w_out.start()
    get_b_out.start()

    stages = {
        f.__name__: f
        for f in (gather, first_product, sum_pieces, activate, second_product, sum_cores, sum_x)
    }
    for name, k in schedule():
        stages[name](k)

    for k, (_, e) in enumerate(PARTS):
        def sent():
            tok_all(k).wait_send()
            sib_copy(k, core).wait_send()
            x_all(k).wait_send()

        on_core(e, sent)
        on_core(None if e is None else 1 - e, lambda: core_copy(k).wait_send())
        pre_all(k).wait_send()
        hid_all(k).wait_send()
        if not PACE or k >= N - PACE:
            half_copy(k).wait_send()
    for d in range(8):
        @pl.when(depth != d)
        def _():
            z_copy(d, d).wait_send()

    acc = out[...] + b_out[...]
    seven = z_recv.at[pl.ds(0, 7)]
    remote(seven, seven, z_ss.at[0], z_rs, at_depth(depth)).wait_recv()
    for s in range(1, 8):
        part = z_recv[(depth + s) % 8].astype(jnp.float32)
        acc = acc + jnp.concatenate([part[:8], part[8:]], axis=1)
    out[...] = acc


def on_device(tokens, weight_in, bias_in, weight_out, bias_out):
    bf16, f32 = jnp.bfloat16, jnp.float32
    dma = pltpu.SemaphoreType.DMA
    vmem = pltpu.VMEM
    summed = pl.pallas_call(
        kernel,
        out_shape=jax.ShapeDtypeStruct((8, WIDTH), f32),
        in_specs=[
            pl.BlockSpec(memory_space=pltpu.HBM),
            pl.BlockSpec(memory_space=pltpu.HBM),
            pl.BlockSpec(memory_space=pltpu.HBM),
            pl.BlockSpec(memory_space=pltpu.HBM),
            pl.BlockSpec(memory_space=pltpu.HBM),
        ],
        out_specs=pl.BlockSpec(memory_space=pltpu.VMEM),
        scratch_shapes=[
            vmem((WIDTH, UNITS), bf16),
            vmem((UNITS, WIDTH), bf16),
            vmem((1, UNITS), f32),
            vmem((1, WIDTH), f32),
            vmem((TOKENS, WIDTH), bf16),
            vmem((TOKENS, UNITS), bf16),
            vmem((TOKENS // 4 * 3, UNITS), bf16),
            vmem((TOKENS, UNITS), f32),
            vmem((TOKENS // 4, UNITS), bf16),
            vmem((TOKENS // 4, UNITS), bf16),
            vmem((TOKENS, UNITS), bf16),
            vmem((TOKENS, WIDTH), f32),
            vmem((N, SIDE, WIDTH), f32),
            vmem((N, 3, MINE, WIDTH), bf16),
            vmem((N, 3, MINE, WIDTH), bf16),
            vmem((N, MINE, WIDTH), f32),
            vmem((8, 16, HALF), bf16),
            vmem((8, 16, HALF), bf16),
            dma((N + 4,)),
            dma((N,)), dma((N,)),
            dma((N,)), dma((N,)),
            dma((N,)), dma((N,)),
            dma((N,)), dma((N,)),
            dma((N,)), dma((N,)),
            dma((N,)), dma((N,)),
            dma((N,)), dma((N,)),
            dma((8,)), dma,
            pltpu.SemaphoreType.REGULAR, pltpu.SemaphoreType.REGULAR,
        ],
        compiler_params=pltpu.CompilerParams(
            collective_id=0, has_side_effects=True, vmem_limit_bytes=60 * 2**20
        ),
        cost_estimate=pl.CostEstimate(
            flops=4 * TOKENS * WIDTH * UNITS, bytes_accessed=4 * WIDTH * UNITS, transcendentals=0
        ),
        name="feed_forward",
    )(tokens, weight_in, bias_in, weight_out, bias_out)
    return summed.astype(jnp.bfloat16)


def solution(mesh):
    placed = (
        P("col", "row"),
        P("row", ("col", "depth")),
        P(("col", "depth")),
        P(("col", "depth"), "row"),
        P("row"),
    )
    return jax.shard_map(
        on_device, mesh=mesh, in_specs=placed, out_specs=P(("col", "depth"), "row"), check_vma=False
    )
```

```python
import jax
import jax.numpy as jnp
from jax import lax
from jax.experimental import pallas as pl
from jax.experimental.pallas import tpu as pltpu
from jax.sharding import PartitionSpec as P

PARTS = tuple((q, e) for q in (0, 1, 3, 2) for e in (1, 0))
N = len(PARTS)
TOKENS, WIDTH, UNITS = 512, 1536, 768
MINE = 16
SIDE = 4 * MINE
SIZES = [SIDE if e is not None else 2 * SIDE for _, e in PARTS]
BASES = [sum(SIZES[:k]) for k in range(N)]
PIECES = [size // 4 for size in SIZES]
TILE = 256
HALF = WIDTH // 2


def schedule():
    before = {"gather": 0, "first_product": 0, "sum_pieces": 2}
    after = {"activate": 0, "second_product": 2, "sum_cores": 3, "sum_x": 5}
    order = []
    for lags in (before, after):
        steps = [(k + lag, n, k) for n, lag in enumerate(lags.values()) for k in range(N)]
        order += [(list(lags)[n], k) for _, n, k in sorted(steps)]
    return order


def remote(src, dst, send, recv, device):
    return pltpu.make_async_remote_copy(
        src_ref=src,
        dst_ref=dst,
        send_sem=send,
        recv_sem=recv,
        device_id=device,
        device_id_type=pl.DeviceIdType.MESH,
    )


def kernel(
    tokens, weight_in, bias_in, weight_out, bias_out, out,
    w_in, w_out, b_in, b_out, gathered, pre_send, pre_recv, pre_sum, pre_out, pre_other, hidden,
    total, total_other, x_send, x_recv, x_sum, z_send, z_recv,
    local_sem, tok_ss, tok_rs, sib_ss, sib_rs, pre_ss, pre_rs, half_ss, half_rs,
    hid_ss, hid_rs, core_ss, core_rs, x_ss, x_rs, z_ss, z_rs, half_ready, depth_ready,
):
    row, col, depth = lax.axis_index("row"), lax.axis_index("col"), lax.axis_index("depth")
    y, z_hi, x, core = row // 2, row % 2, col // 2, col % 2

    def at_x(step):
        return {"col": ((x + step) % 4) * 2 + core}

    def at_y(step):
        return {"row": ((y + step) % 4) * 2 + z_hi}

    sibling = {"col": x * 2 + 1 - core}
    other_half = {"row": y * 2 + 1 - z_hi}

    def at_depth(d):
        return {"depth": d}

    def on_core(e, body):
        if e is None:
            body()
        else:
            pl.when(core == e)(body)

    def rows(start, size):
        return pl.ds(pl.multiple_of(start, 16), size)

    def core_rows(k, which):
        return rows(BASES[k] + (which * SIDE if PARTS[k][1] is None else 0), SIDE)

    def own_rows(k):
        return rows(BASES[k] + (core * SIDE if PARTS[k][1] is None else 0) + x * MINE, MINE)

    get_w_in = pltpu.make_async_copy(weight_in, w_in, local_sem.at[N])
    get_w_out = pltpu.make_async_copy(weight_out, w_out, local_sem.at[N + 1])
    get_b_in = pltpu.make_async_copy(bias_in, b_in.at[0], local_sem.at[N + 2])
    get_b_out = pltpu.make_async_copy(bias_out, b_out.at[0], local_sem.at[N + 3])
    get_own = [
        pltpu.make_async_copy(
            tokens.at[pl.ds(q * MINE, MINE)], gathered.at[own_rows(k)], local_sem.at[k]
        )
        for k, (q, _) in enumerate(PARTS)
    ]
    for k, (_, e) in enumerate(PARTS):
        on_core(e, get_own[k].start)
    get_w_in.start()
    get_b_in.start()

    def signal(semaphore, device):
        pl.semaphore_signal(
            semaphore, inc=1, device_id=device, device_id_type=pl.DeviceIdType.MESH
        )

    barrier = pltpu.get_barrier_semaphore()
    near = [at_x(1), at_x(2), at_x(3), at_y(1), at_y(2), at_y(3), sibling]
    for device in near:
        signal(barrier, device)

    @pl.when(z_hi == 0)
    def _():
        signal(barrier, other_half)

    for d in range(1, 8):
        @pl.when(depth < d)
        def _():
            signal(barrier, at_depth(d))

    pl.semaphore_wait(barrier, len(near) + z_hi + depth)

    def tok_copy(k, s):
        src = tokens.at[pl.ds(PARTS[k][0] * MINE, MINE)]
        return remote(src, gathered.at[own_rows(k)], tok_ss.at[k], tok_rs.at[k], at_x(s))

    def tok_all(k):
        place = gathered.at[pl.ds(BASES[k], 3 * MINE)]
        return remote(place, place, tok_ss.at[k], tok_rs.at[k], at_x(1))

    def sib_copy(k, which):
        place = gathered.at[core_rows(k, which)]
        return remote(place, place, sib_ss.at[k], sib_rs.at[k], sibling)

    def pre_slot(k, s):
        return pre_recv.at[pl.ds(BASES[k] // 4 * 3 + (s - 1) * PIECES[k], PIECES[k])]

    def pre_copy(k, s):
        piece = rows(BASES[k] + ((y + s) % 4) * PIECES[k], PIECES[k])
        return remote(pre_send.at[piece], pre_slot(k, s), pre_ss.at[k], pre_rs.at[k], at_y(s))

    def pre_all(k):
        place = pre_recv.at[pl.ds(BASES[k] // 4 * 3, 3 * PIECES[k])]
        return remote(place, place, pre_ss.at[k], pre_rs.at[k], at_y(1))

    def half_copy(k):
        piece = pl.ds(BASES[k] // 4, PIECES[k])
        return remote(
            pre_out.at[piece], pre_other.at[piece], half_ss.at[k], half_rs.at[k], other_half
        )

    def my_piece(k):
        return rows(BASES[k] + y * PIECES[k], PIECES[k])

    def hid_copy(k, s):
        place = hidden.at[my_piece(k)]
        return remote(place, place, hid_ss.at[k], hid_rs.at[k], at_y(s))

    def hid_all(k):
        place = hidden.at[pl.ds(BASES[k], 3 * PIECES[k])]
        return remote(place, place, hid_ss.at[k], hid_rs.at[k], at_y(1))

    def core_copy(k):
        return remote(
            total.at[core_rows(k, 1 - core)], total_other.at[k], core_ss.at[k], core_rs.at[k], sibling
        )

    def x_copy(k, s):
        return remote(x_send.at[k, s - 1], x_recv.at[k, s - 1], x_ss.at[k], x_rs.at[k], at_x(s))

    def x_all(k):
        return remote(x_send.at[k], x_recv.at[k], x_ss.at[k], x_rs.at[k], at_x(1))

    def z_copy(d, to):
        return remote(z_send.at[d], z_recv.at[depth], z_ss.at[d], z_rs, at_depth(to))

    def gather(k):
        e = PARTS[k][1]

        def body():
            get_own[k].wait()
            tok_all(k).wait_recv()
            sib_copy(k, core).start()

        on_core(e, body)

    def first_product(k):
        e = PARTS[k][1]
        on_core(None if e is None else 1 - e, lambda: sib_copy(k, 1 - core).wait_recv())
        if k == 0:
            get_w_in.wait()
            get_b_in.wait()
        part_rows = pl.ds(BASES[k], SIZES[k])

        def tile(i, _):
            units = pl.ds(pl.multiple_of(i * TILE, TILE), TILE)
            part = jnp.dot(
                gathered[part_rows, :], w_in[:, units], preferred_element_type=jnp.float32
            )
            pre_send[part_rows, units] = part.astype(jnp.bfloat16)
            pre_sum[part_rows, units] = part
            return 0

        lax.fori_loop(0, UNITS // TILE, tile, 0)
        for s in range(1, 4):
            pre_copy(k, s).start()

    def sum_pieces(k):
        acc = pre_sum[my_piece(k), :]
        pre_all(k).wait_recv()
        for s in range(1, 4):
            acc = acc + pre_slot(k, s)[...].astype(jnp.float32)
        pre_out[pl.ds(BASES[k] // 4, PIECES[k]), :] = acc.astype(jnp.bfloat16)
        if k == 0:
            @pl.when(z_hi == 0)
            def _():
                pl.semaphore_wait(half_ready, 1)

        half_copy(k).start()
        pre_sum[my_piece(k), :] = acc

    def activate(k):
        acc = pre_sum[my_piece(k), :] + b_in[...]
        half_copy(k).wait_recv()
        v = acc + pre_other[pl.ds(BASES[k] // 4, PIECES[k]), :].astype(jnp.float32)
        hidden[my_piece(k), :] = jax.nn.gelu(v, approximate=True).astype(jnp.bfloat16)
        for s in range(1, 4):
            hid_copy(k, s).start()

    def second_product(k):
        hid_all(k).wait_recv()
        if k == 0:
            get_w_out.wait()
            get_b_out.wait()
        part_rows = pl.ds(BASES[k], SIZES[k])

        def tile(i, _):
            cols = pl.ds(pl.multiple_of(i * TILE, TILE), TILE)
            total[part_rows, cols] = jnp.dot(
                hidden[part_rows, :], w_out[:, cols], preferred_element_type=jnp.float32
            )
            return 0

        lax.fori_loop(0, WIDTH // TILE, tile, 0)
        e = PARTS[k][1]
        on_core(None if e is None else 1 - e, lambda: core_copy(k).start())

    def sum_cores(k):
        e = PARTS[k][1]
        first = BASES[k] + (core * SIDE if e is None else 0)

        def body():
            core_copy(k).wait_recv()
            for s in (2, 1, 3, 0):
                i = (x + s) % 4
                part = total[rows(first + i * MINE, MINE), :] + total_other[k, rows(i * MINE, MINE), :]
                if s:
                    x_send[k, s - 1] = part.astype(jnp.bfloat16)
                    x_copy(k, s).start()
                else:
                    x_sum[k] = part

        on_core(e, body)

    def sum_x(k):
        q, e = PARTS[k]
        if k == 0:
            @pl.when(depth < 7)
            def _():
                pl.semaphore_wait(depth_ready, 7 - depth)

        def body():
            acc = x_sum[k]
            x_all(k).wait_recv()
            for s in range(1, 4):
                acc = acc + x_recv[k, s - 1].astype(jnp.float32)
            for n in range(2):
                d = 2 * q + n
                part = acc[n * 8:(n + 1) * 8]
                folded = jnp.concatenate([part[:, :HALF], part[:, HALF:]], axis=0)

                @pl.when(depth == d)
                def _():
                    out[...] = part

                @pl.when(depth != d)
                def _():
                    z_send[d] = folded.astype(jnp.bfloat16)
                    z_copy(d, d).start()

        on_core(e, body)

    def send_tokens(k):
        for s in (2, 1, 3):
            tok_copy(k, s).start()

    for k, (_, e) in enumerate(PARTS):
        on_core(e, lambda: send_tokens(k))

    @pl.when(z_hi == 1)
    def _():
        signal(half_ready, other_half)

    for d in range(7):
        @pl.when(depth > d)
        def _():
            signal(depth_ready, at_depth(d))

    get_w_out.start()
    get_b_out.start()

    stages = {
        f.__name__: f
        for f in (gather, first_product, sum_pieces, activate, second_product, sum_cores, sum_x)
    }
    for name, k in schedule():
        stages[name](k)

    for k, (_, e) in enumerate(PARTS):
        def sent():
            tok_all(k).wait_send()
            sib_copy(k, core).wait_send()
            x_all(k).wait_send()

        on_core(e, sent)
        on_core(None if e is None else 1 - e, lambda: core_copy(k).wait_send())
        pre_all(k).wait_send()
        hid_all(k).wait_send()
        half_copy(k).wait_send()
    for d in range(8):
        @pl.when(depth != d)
        def _():
            z_copy(d, d).wait_send()

    acc = out[...] + b_out[...]
    seven = z_recv.at[pl.ds(0, 7)]
    remote(seven, seven, z_ss.at[0], z_rs, at_depth(depth)).wait_recv()
    for s in range(1, 8):
        part = z_recv[(depth + s) % 8].astype(jnp.float32)
        acc = acc + jnp.concatenate([part[:8], part[8:]], axis=1)
    out[...] = acc


def on_device(tokens, weight_in, bias_in, weight_out, bias_out):
    bf16, f32 = jnp.bfloat16, jnp.float32
    dma = pltpu.SemaphoreType.DMA
    vmem = pltpu.VMEM
    summed = pl.pallas_call(
        kernel,
        out_shape=jax.ShapeDtypeStruct((8, WIDTH), f32),
        in_specs=[
            pl.BlockSpec(memory_space=pltpu.HBM),
            pl.BlockSpec(memory_space=pltpu.HBM),
            pl.BlockSpec(memory_space=pltpu.HBM),
            pl.BlockSpec(memory_space=pltpu.HBM),
            pl.BlockSpec(memory_space=pltpu.HBM),
        ],
        out_specs=pl.BlockSpec(memory_space=pltpu.VMEM),
        scratch_shapes=[
            vmem((WIDTH, UNITS), bf16),
            vmem((UNITS, WIDTH), bf16),
            vmem((1, UNITS), f32),
            vmem((1, WIDTH), f32),
            vmem((TOKENS, WIDTH), bf16),
            vmem((TOKENS, UNITS), bf16),
            vmem((TOKENS // 4 * 3, UNITS), bf16),
            vmem((TOKENS, UNITS), f32),
            vmem((TOKENS // 4, UNITS), bf16),
            vmem((TOKENS // 4, UNITS), bf16),
            vmem((TOKENS, UNITS), bf16),
            vmem((TOKENS, WIDTH), f32),
            vmem((N, SIDE, WIDTH), f32),
            vmem((N, 3, MINE, WIDTH), bf16),
            vmem((N, 3, MINE, WIDTH), bf16),
            vmem((N, MINE, WIDTH), f32),
            vmem((8, 16, HALF), bf16),
            vmem((8, 16, HALF), bf16),
            dma((N + 4,)),
            dma((N,)), dma((N,)),
            dma((N,)), dma((N,)),
            dma((N,)), dma((N,)),
            dma((N,)), dma((N,)),
            dma((N,)), dma((N,)),
            dma((N,)), dma((N,)),
            dma((N,)), dma((N,)),
            dma((8,)), dma,
            pltpu.SemaphoreType.REGULAR, pltpu.SemaphoreType.REGULAR,
        ],
        compiler_params=pltpu.CompilerParams(
            collective_id=0, has_side_effects=True, vmem_limit_bytes=60 * 2**20
        ),
        cost_estimate=pl.CostEstimate(
            flops=4 * TOKENS * WIDTH * UNITS, bytes_accessed=4 * WIDTH * UNITS, transcendentals=0
        ),
        name="feed_forward",
    )(tokens, weight_in, bias_in, weight_out, bias_out)
    return summed.astype(jnp.bfloat16)


def solution(mesh):
    placed = (
        P("col", "row"),
        P("row", ("col", "depth")),
        P(("col", "depth")),
        P(("col", "depth"), "row"),
        P("row"),
    )
    return jax.shard_map(
        on_device, mesh=mesh, in_specs=placed, out_specs=P(("col", "depth"), "row"), check_vma=False
    )
```

```python
import jax
import jax.numpy as jnp
from jax import lax
from jax.experimental import pallas as pl
from jax.experimental.pallas import tpu as pltpu
from jax.sharding import PartitionSpec as P

PARTS = tuple((q, e) for q in (0, 1, 3, 2) for e in (1, 0))
N = len(PARTS)
TOKENS, WIDTH, UNITS = 512, 1536, 768
MINE = 16
SIDE = 4 * MINE
SIZES = [SIDE if e is not None else 2 * SIDE for _, e in PARTS]
BASES = [sum(SIZES[:k]) for k in range(N)]
PIECES = [size // 4 for size in SIZES]
TILE = 256
AHEAD = 3
HALF = WIDTH // 2


def schedule():
    lags = {
        "gather": 0, "first_product": 0, "sum_pieces": 2,
        "activate": 7, "second_product": 9, "sum_cores": 10, "sum_x": 12,
    }
    steps = sorted((k + lag, n, k) for n, lag in enumerate(lags.values()) for k in range(N))
    order = [(list(lags)[n], k) for _, n, k in steps]
    return order


def remote(src, dst, send, recv, device):
    return pltpu.make_async_remote_copy(
        src_ref=src,
        dst_ref=dst,
        send_sem=send,
        recv_sem=recv,
        device_id=device,
        device_id_type=pl.DeviceIdType.MESH,
    )


def kernel(
    tokens, weight_in, bias_in, weight_out, bias_out, out,
    w_in, w_out, b_in, b_out, gathered, pre_send, pre_recv, pre_sum, pre_out, pre_other, hidden,
    total, total_other, x_send, x_recv, x_sum, z_send, z_recv,
    local_sem, tok_ss, tok_rs, sib_ss, sib_rs, pre_ss, pre_rs, half_ss, half_rs,
    hid_ss, hid_rs, core_ss, core_rs, x_ss, x_rs, z_ss, z_rs, half_ready, depth_ready,
):
    row, col, depth = lax.axis_index("row"), lax.axis_index("col"), lax.axis_index("depth")
    y, z_hi, x, core = row // 2, row % 2, col // 2, col % 2

    def at_x(step):
        return {"col": ((x + step) % 4) * 2 + core}

    def at_y(step):
        return {"row": ((y + step) % 4) * 2 + z_hi}

    sibling = {"col": x * 2 + 1 - core}
    other_half = {"row": y * 2 + 1 - z_hi}

    def at_depth(d):
        return {"depth": d}

    def on_core(e, body):
        if e is None:
            body()
        else:
            pl.when(core == e)(body)

    def rows(start, size):
        return pl.ds(pl.multiple_of(start, 16), size)

    def core_rows(k, which):
        return rows(BASES[k] + (which * SIDE if PARTS[k][1] is None else 0), SIDE)

    def own_rows(k):
        return rows(BASES[k] + (core * SIDE if PARTS[k][1] is None else 0) + x * MINE, MINE)

    get_w_in = pltpu.make_async_copy(weight_in, w_in, local_sem.at[N])
    get_w_out = pltpu.make_async_copy(weight_out, w_out, local_sem.at[N + 1])
    get_b_in = pltpu.make_async_copy(bias_in, b_in.at[0], local_sem.at[N + 2])
    get_b_out = pltpu.make_async_copy(bias_out, b_out.at[0], local_sem.at[N + 3])
    get_own = [
        pltpu.make_async_copy(
            tokens.at[pl.ds(q * MINE, MINE)], gathered.at[own_rows(k)], local_sem.at[k]
        )
        for k, (q, _) in enumerate(PARTS)
    ]
    for k, (_, e) in enumerate(PARTS):
        on_core(e, get_own[k].start)
    get_w_in.start()
    get_b_in.start()

    def signal(semaphore, device):
        pl.semaphore_signal(
            semaphore, inc=1, device_id=device, device_id_type=pl.DeviceIdType.MESH
        )

    barrier = pltpu.get_barrier_semaphore()
    near = [at_x(1), at_x(2), at_x(3), at_y(1), at_y(2), at_y(3), sibling]
    for device in near:
        signal(barrier, device)

    @pl.when(z_hi == 0)
    def _():
        signal(barrier, other_half)

    for d in range(1, 8):
        @pl.when(depth < d)
        def _():
            signal(barrier, at_depth(d))

    pl.semaphore_wait(barrier, len(near) + z_hi + depth)

    def tok_copy(k, s):
        src = tokens.at[pl.ds(PARTS[k][0] * MINE, MINE)]
        return remote(src, gathered.at[own_rows(k)], tok_ss.at[k], tok_rs.at[k], at_x(s))

    def tok_all(k):
        place = gathered.at[pl.ds(BASES[k], 3 * MINE)]
        return remote(place, place, tok_ss.at[k], tok_rs.at[k], at_x(1))

    def sib_copy(k, which):
        place = gathered.at[core_rows(k, which)]
        return remote(place, place, sib_ss.at[k], sib_rs.at[k], sibling)

    def pre_slot(k, s):
        return pre_recv.at[pl.ds(BASES[k] // 4 * 3 + (s - 1) * PIECES[k], PIECES[k])]

    def pre_copy(k, s):
        piece = rows(BASES[k] + ((y + s) % 4) * PIECES[k], PIECES[k])
        return remote(pre_send.at[piece], pre_slot(k, s), pre_ss.at[k], pre_rs.at[k], at_y(s))

    def pre_all(k):
        place = pre_recv.at[pl.ds(BASES[k] // 4 * 3, 3 * PIECES[k])]
        return remote(place, place, pre_ss.at[k], pre_rs.at[k], at_y(1))

    def half_copy(k):
        piece = pl.ds(BASES[k] // 4, PIECES[k])
        return remote(
            pre_out.at[piece], pre_other.at[piece], half_ss.at[k], half_rs.at[k], other_half
        )

    def my_piece(k):
        return rows(BASES[k] + y * PIECES[k], PIECES[k])

    def hid_copy(k, s):
        place = hidden.at[my_piece(k)]
        return remote(place, place, hid_ss.at[k], hid_rs.at[k], at_y(s))

    def hid_all(k):
        place = hidden.at[pl.ds(BASES[k], 3 * PIECES[k])]
        return remote(place, place, hid_ss.at[k], hid_rs.at[k], at_y(1))

    def core_copy(k):
        return remote(
            total.at[core_rows(k, 1 - core)], total_other.at[k], core_ss.at[k], core_rs.at[k], sibling
        )

    def x_copy(k, s):
        return remote(x_send.at[k, s - 1], x_recv.at[k, s - 1], x_ss.at[k], x_rs.at[k], at_x(s))

    def x_all(k):
        return remote(x_send.at[k], x_recv.at[k], x_ss.at[k], x_rs.at[k], at_x(1))

    def z_copy(d, to):
        return remote(z_send.at[d], z_recv.at[depth], z_ss.at[d], z_rs, at_depth(to))

    def send_tokens(k):
        for s in (2, 1, 3):
            tok_copy(k, s).start()

    def gather(k):
        e = PARTS[k][1]

        def body():
            get_own[k].wait()
            tok_all(k).wait_recv()
            sib_copy(k, core).start()

        on_core(e, body)
        if k + AHEAD < N:
            on_core(PARTS[k + AHEAD][1], lambda: send_tokens(k + AHEAD))

    def first_product(k):
        e = PARTS[k][1]
        on_core(None if e is None else 1 - e, lambda: sib_copy(k, 1 - core).wait_recv())
        if k == 0:
            get_w_in.wait()
            get_b_in.wait()
        part_rows = pl.ds(BASES[k], SIZES[k])

        def tile(i, _):
            units = pl.ds(pl.multiple_of(i * TILE, TILE), TILE)
            part = jnp.dot(
                gathered[part_rows, :], w_in[:, units], preferred_element_type=jnp.float32
            )
            pre_send[part_rows, units] = part.astype(jnp.bfloat16)
            pre_sum[part_rows, units] = part
            return 0

        lax.fori_loop(0, UNITS // TILE, tile, 0)
        for s in range(1, 4):
            pre_copy(k, s).start()

    def sum_pieces(k):
        acc = pre_sum[my_piece(k), :]
        pre_all(k).wait_recv()
        for s in range(1, 4):
            acc = acc + pre_slot(k, s)[...].astype(jnp.float32)
        pre_out[pl.ds(BASES[k] // 4, PIECES[k]), :] = acc.astype(jnp.bfloat16)
        if k == 0:
            @pl.when(z_hi == 0)
            def _():
                pl.semaphore_wait(half_ready, 1)

        half_copy(k).start()
        pre_sum[my_piece(k), :] = acc

    def activate(k):
        acc = pre_sum[my_piece(k), :] + b_in[...]
        half_copy(k).wait_recv()
        v = acc + pre_other[pl.ds(BASES[k] // 4, PIECES[k]), :].astype(jnp.float32)
        hidden[my_piece(k), :] = jax.nn.gelu(v, approximate=True).astype(jnp.bfloat16)
        for s in range(1, 4):
            hid_copy(k, s).start()

    def second_product(k):
        hid_all(k).wait_recv()
        if k == 0:
            get_w_out.wait()
            get_b_out.wait()
        part_rows = pl.ds(BASES[k], SIZES[k])

        def tile(i, _):
            cols = pl.ds(pl.multiple_of(i * TILE, TILE), TILE)
            total[part_rows, cols] = jnp.dot(
                hidden[part_rows, :], w_out[:, cols], preferred_element_type=jnp.float32
            )
            return 0

        lax.fori_loop(0, WIDTH // TILE, tile, 0)
        e = PARTS[k][1]
        on_core(None if e is None else 1 - e, lambda: core_copy(k).start())

    def sum_cores(k):
        e = PARTS[k][1]
        first = BASES[k] + (core * SIDE if e is None else 0)

        def body():
            core_copy(k).wait_recv()
            for s in (2, 1, 3, 0):
                i = (x + s) % 4
                part = total[rows(first + i * MINE, MINE), :] + total_other[k, rows(i * MINE, MINE), :]
                if s:
                    x_send[k, s - 1] = part.astype(jnp.bfloat16)
                    x_copy(k, s).start()
                else:
                    x_sum[k] = part

        on_core(e, body)

    def sum_x(k):
        q, e = PARTS[k]
        if k == 0:
            @pl.when(depth < 7)
            def _():
                pl.semaphore_wait(depth_ready, 7 - depth)

        def body():
            acc = x_sum[k]
            x_all(k).wait_recv()
            for s in range(1, 4):
                acc = acc + x_recv[k, s - 1].astype(jnp.float32)
            for n in range(2):
                d = 2 * q + n
                part = acc[n * 8:(n + 1) * 8]
                folded = jnp.concatenate([part[:, :HALF], part[:, HALF:]], axis=0)

                @pl.when(depth == d)
                def _():
                    out[...] = part

                @pl.when(depth != d)
                def _():
                    z_send[d] = folded.astype(jnp.bfloat16)
                    z_copy(d, d).start()

        on_core(e, body)

    for k in range(AHEAD):
        on_core(PARTS[k][1], lambda: send_tokens(k))

    @pl.when(z_hi == 1)
    def _():
        signal(half_ready, other_half)

    for d in range(7):
        @pl.when(depth > d)
        def _():
            signal(depth_ready, at_depth(d))

    get_w_out.start()
    get_b_out.start()

    stages = {
        f.__name__: f
        for f in (gather, first_product, sum_pieces, activate, second_product, sum_cores, sum_x)
    }
    for name, k in schedule():
        stages[name](k)

    for k, (_, e) in enumerate(PARTS):
        def sent():
            tok_all(k).wait_send()
            sib_copy(k, core).wait_send()
            x_all(k).wait_send()

        on_core(e, sent)
        on_core(None if e is None else 1 - e, lambda: core_copy(k).wait_send())
        pre_all(k).wait_send()
        hid_all(k).wait_send()
        half_copy(k).wait_send()
    for d in range(8):
        @pl.when(depth != d)
        def _():
            z_copy(d, d).wait_send()

    acc = out[...] + b_out[...]
    seven = z_recv.at[pl.ds(0, 7)]
    remote(seven, seven, z_ss.at[0], z_rs, at_depth(depth)).wait_recv()
    for s in range(1, 8):
        part = z_recv[(depth + s) % 8].astype(jnp.float32)
        acc = acc + jnp.concatenate([part[:8], part[8:]], axis=1)
    out[...] = acc


def on_device(tokens, weight_in, bias_in, weight_out, bias_out):
    bf16, f32 = jnp.bfloat16, jnp.float32
    dma = pltpu.SemaphoreType.DMA
    vmem = pltpu.VMEM
    summed = pl.pallas_call(
        kernel,
        out_shape=jax.ShapeDtypeStruct((8, WIDTH), f32),
        in_specs=[
            pl.BlockSpec(memory_space=pltpu.HBM),
            pl.BlockSpec(memory_space=pltpu.HBM),
            pl.BlockSpec(memory_space=pltpu.HBM),
            pl.BlockSpec(memory_space=pltpu.HBM),
            pl.BlockSpec(memory_space=pltpu.HBM),
        ],
        out_specs=pl.BlockSpec(memory_space=pltpu.VMEM),
        scratch_shapes=[
            vmem((WIDTH, UNITS), bf16),
            vmem((UNITS, WIDTH), bf16),
            vmem((1, UNITS), f32),
            vmem((1, WIDTH), f32),
            vmem((TOKENS, WIDTH), bf16),
            vmem((TOKENS, UNITS), bf16),
            vmem((TOKENS // 4 * 3, UNITS), bf16),
            vmem((TOKENS, UNITS), f32),
            vmem((TOKENS // 4, UNITS), bf16),
            vmem((TOKENS // 4, UNITS), bf16),
            vmem((TOKENS, UNITS), bf16),
            vmem((TOKENS, WIDTH), f32),
            vmem((N, SIDE, WIDTH), f32),
            vmem((N, 3, MINE, WIDTH), bf16),
            vmem((N, 3, MINE, WIDTH), bf16),
            vmem((N, MINE, WIDTH), f32),
            vmem((8, 16, HALF), bf16),
            vmem((8, 16, HALF), bf16),
            dma((N + 4,)),
            dma((N,)), dma((N,)),
            dma((N,)), dma((N,)),
            dma((N,)), dma((N,)),
            dma((N,)), dma((N,)),
            dma((N,)), dma((N,)),
            dma((N,)), dma((N,)),
            dma((N,)), dma((N,)),
            dma((8,)), dma,
            pltpu.SemaphoreType.REGULAR, pltpu.SemaphoreType.REGULAR,
        ],
        compiler_params=pltpu.CompilerParams(
            collective_id=0, has_side_effects=True, vmem_limit_bytes=60 * 2**20
        ),
        cost_estimate=pl.CostEstimate(
            flops=4 * TOKENS * WIDTH * UNITS, bytes_accessed=4 * WIDTH * UNITS, transcendentals=0
        ),
        name="feed_forward",
    )(tokens, weight_in, bias_in, weight_out, bias_out)
    return summed.astype(jnp.bfloat16)


def solution(mesh):
    placed = (
        P("col", "row"),
        P("row", ("col", "depth")),
        P(("col", "depth")),
        P(("col", "depth"), "row"),
        P("row"),
    )
    return jax.shard_map(
        on_device, mesh=mesh, in_specs=placed, out_specs=P(("col", "depth"), "row"), check_vma=False
    )
```
